32 devices in a mesh: grp: 2 (over y), ae: 4 (over z), tp: 2 (over x), sub: 2 (over core).
Axes of the slice: x: 2, y: 2, z: 4, core: 2. Of those that a mesh axis runs over, the one named last changes fastest.
Arguments:
- tokens: bfloat16 [256, 3072], P(('grp', 'ae', 'sub'), 'tp'), parts along dimension 0
- queries: bfloat16 [256, 3072], P(('grp', 'ae', 'sub'), 'tp'), parts along dimension 0, may hold values from -2 to 2
- kv_cache: bfloat16 [2, 256, 8, 64, 128], P(None, ('grp', 'ae', 'sub'), 'tp'), parts along dimension 1, may hold values from -2 to 2
- new_kv: bfloat16 [2, 256, 1024], P(None, ('grp', 'ae', 'sub'), 'tp'), parts along dimension 1, may hold values from -2 to 2
- lengths: int32 [256], P(('grp', 'ae', 'sub')), parts along dimension 0, may hold values from 1 to 64
- routes: int32 [256, 4], P(('grp', 'ae', 'sub')), parts along dimension 0, may hold values from 0 to 15, all different within a row; in each aligned block of 16 rows (0 to 15, 16 to 31, ...) at most 5 rows name the same one
- placement: int32 [16], replicated, may hold values from 0 to 15, each once
- router_weight: bfloat16 [3072, 16], replicated, may hold values from -0.109375 to 0.109375
- w_up: bfloat16 [16, 3072, 5376], P('ae', None, ('tp', 'sub')), may hold values from -0.109375 to 0.109375
- w_down: bfloat16 [16, 5376, 3072], P('ae', ('tp', 'sub')), may hold values from -0.109375 to 0.109375
Outputs:
- expert_mix: bfloat16 [256, 3072], P(('grp', 'ae', 'sub'), 'tp'), parts along dimension 0
The draws below stay inside these ranges and needn't reach their ends.
There are 2 independent parts, one for each index of `grp`. The reference program is written for one: setup_inputs(seed, part) draws one part's arguments, and reference() takes and returns one part's arrays. A program takes and returns all parts, laid end to end along the dimension named above; an argument that names none is the same for every part. Nothing has to cross between parts.
Inputs may be any that keep to these rules, and one draw needn't show every extreme that they name: `routes`: each row names 4 different experts. In each aligned block of 16 rows (the rows of one device) no expert is named by more than 5 rows, and in some block one expert is named by exactly 5 rows. A permutation: expert e uses entry placement[e] of w_up and w_down.
All inputs are finite; a program needn't handle non-finite values.
Results may differ from the reference program's by a relative error of at most 0.0085.
Values may be sent and summed in bfloat16 or wider, within the bound.
No kernel may reach another device: no remote copies, remote signals or barrier semaphores. Data moves between devices by JAX's collectives and lax.ppermute only.
A program may use at most 256 MiB of HBM per device.

```python
import math
import jax
import jax.numpy as jnp
import numpy as np
from jax import lax

ROW_DEV = 16
CTX = 64
HD = 128
KVH = 8
QH = 24
F = 5376
E = 16
TOP = 4
D = 3072
CAP = 5
ROWS = 128


def draw_tokens(key, part):
    key = jax.random.fold_in(key, 11)
    row_key, column_key, value_key = jax.random.split(key, 3)
    columns = jnp.arange(D, dtype=jnp.float32) / D
    jitter = jnp.exp(jax.random.uniform(column_key, (D,), jnp.float32, -0.5, 0.5))
    values = jax.random.normal(value_key, (ROWS, D), jnp.float32)
    row_scale = jnp.exp(jax.random.uniform(row_key, (ROWS, 1), jnp.float32, math.log(0.3), math.log(3.0)))
    column_scale = 0.3 * jnp.exp(math.log(10.0) * columns) * jitter
    return (values * row_scale * column_scale[None, :]).astype(jnp.bfloat16)


def set_ends(values, key, low, top_value):
    dims = values.shape
    place = [jax.random.randint(jax.random.fold_in(key, axis), (), 0, dims[axis]) for axis in range(len(dims))]
    values = values.at[tuple(place)].set(low)
    longest = dims.index(max(dims))
    place[longest] = (place[longest] + 1) % dims[longest]
    return values.at[tuple(place)].set(top_value)


def strengthened(entries, key, source, target, parts, factor):
    def block_of(dim):
        return (jnp.arange(entries.shape[dim]) // (entries.shape[dim] // parts)).reshape((-1,) + (1,) * (entries.ndim - 1 - dim))

    near = jax.random.permutation(key, parts)[block_of(target)]
    second = (block_of(target) + parts // 2) % parts
    return jnp.where((block_of(source) == near) | (block_of(source) == second), factor * entries, entries)


def levels(rng, dims, cuts, least, high):
    def one(axis_at, shards_of):
        heights = jax.random.uniform(jax.random.fold_in(jax.random.fold_in(rng, 6), axis_at), (shards_of,), jnp.float32, least / len(cuts), high / len(cuts))
        return jnp.repeat(jnp.exp(heights), dims[axis_at] // shards_of).reshape((-1,) + (1,) * (len(dims) - axis_at - 1))

    factor_of = one(*cuts[0])
    for cut in cuts[1:]:
        factor_of = factor_of * one(*cut)
    return factor_of


def shared_out(stream_key, own, number, rows, amount, top, limit, slope):
    sequence = jax.random.permutation(stream_key, amount)
    packed, common = load_shares(amount, rows * top, limit, slope, True), load_shares(amount, rows * top, limit, slope, False)
    places = jnp.arange(amount)

    def named(tallies, rotation):
        used = int((tallies > 0).sum())
        fixed = max(1, used // 4)
        moved = fixed + (places - fixed + rotation * (used - fixed)) % max(1, amount - fixed)
        return jnp.zeros((amount,), jnp.int32).at[sequence[jnp.where(places < fixed, places, moved)]].set(jnp.asarray(tallies, jnp.int32))

    tallies = jnp.where(number % 4 == 0, named(packed, number // 4), named(common, number - number // 4 - 1))
    mixed = jax.random.permutation(jax.random.fold_in(own, 3), amount)
    source_of, taker = mixed[0:amount // 2 * 2:2], mixed[1:amount // 2 * 2:2]
    slack = jnp.minimum(tallies[source_of] - 1, limit - tallies[taker]) // 2
    slack = jnp.where((source_of == sequence[0]) | (taker == sequence[0]) | (tallies[taker] == 0), 0, jnp.maximum(slack, 0))
    moved = jax.random.randint(jax.random.fold_in(own, 4), (amount // 2,), 0, 1 << 20) % (slack + 1)
    tallies = tallies.at[source_of].add(-moved).at[taker].add(moved)
    members = jnp.searchsorted(jnp.cumsum(tallies), jnp.arange(rows * top), side="right").astype(jnp.int32)
    listing = members.reshape(top, rows).T
    listing = listing[jax.random.permutation(jax.random.fold_in(own, 1), rows)]
    rotation = jax.random.randint(jax.random.fold_in(own, 2), (rows, 1), 0, top)
    return jnp.take_along_axis(listing, (jnp.arange(top)[None, :] + rotation) % top, axis=1)


def load_shares(amount, total, limit, slope, full):
    weights = [(1 << 20) // math.isqrt(grade ** slope) + 1 for grade in range(1, amount + 1)]
    largest = limit if full else min(limit, max(-(-total // amount), total * weights[0] // sum(weights)))
    least = 1 if total - largest >= amount - 1 else 0
    given, surplus = [largest] + [least] * (amount - 1), total - largest - least * (amount - 1)
    while surplus > 0:
        candidates = [i for i in range(1, amount) if given[i] < largest] or [i for i in range(1, amount) if given[i] < limit]
        pool, budget = sum([weights[i] for i in candidates]), surplus
        for i in candidates:
            more = min(limit - given[i], max(1, budget * weights[i] // pool), surplus)
            given[i] = given[i] + more
            surplus = surplus - more
    return np.array(given)


def bell_draw(own_key, shape, width, most, shards=(), kind=jnp.bfloat16):
    drawn = width * jax.random.normal(own_key, shape, jnp.float32)
    if shards:
        drawn = drawn * levels(own_key, shape, shards, -0.22, 0.18)
    return jnp.clip(drawn, -most, most).astype(kind)


def noise_with(rng, extent, scale, limit, cuts, heavy, kind=jnp.bfloat16):
    drawn = scale * jax.random.normal(rng, extent, jnp.float32)
    if cuts:
        drawn = drawn * levels(rng, extent, cuts, -0.22, 0.18)
    return jnp.clip(strengthened(drawn, jax.random.fold_in(rng, 3), *heavy), -limit, limit).astype(kind)


def setup_inputs(seed: int = 0, part: int = 0) -> dict:
    key_list = jax.random.split(jax.random.key(seed), 11)
    own_keys = jax.random.split(jax.random.fold_in(key_list[10], part), 11)
    tokens = draw_tokens(jax.random.fold_in(jax.random.fold_in(key_list[10], part), 71), part)
    queries = jnp.clip(jax.random.uniform(own_keys[1], (ROWS, D), jnp.float32, -2.0, 2.0) * levels(own_keys[1], (ROWS, D), ((0, 8), (1, 2)), -0.4, 0.0), -2.0, 2.0).astype(jnp.bfloat16)
    kv_cache = jnp.clip(jax.random.uniform(own_keys[2], (2, ROWS, KVH, CTX, HD), jnp.float32, -2.0, 2.0) * levels(own_keys[2], (2, ROWS, KVH, CTX, HD), ((1, 8), (2, 2)), -0.4, 0.0), -2.0, 2.0).astype(jnp.bfloat16)
    new_kv = jnp.clip(jax.random.uniform(own_keys[3], (2, ROWS, KVH * HD), jnp.float32, -2.0, 2.0) * levels(own_keys[3], (2, ROWS, KVH * HD), ((1, 8), (2, 2)), -0.4, 0.0), -2.0, 2.0).astype(jnp.bfloat16)
    lengths = set_ends(jax.random.randint(own_keys[4], (ROWS,), 1, CTX + 1), jax.random.fold_in(own_keys[4], 1), 1, CTX).astype(jnp.int32)
    routes_keys = jax.random.split(jax.random.fold_in(own_keys[5], 1), ROWS // ROW_DEV)
    routes_turns = jax.random.permutation(jax.random.fold_in(own_keys[5], 3), ROWS // ROW_DEV)
    routes = jax.vmap(lambda own, number: shared_out(jax.random.fold_in(own_keys[5], 2), own, number, ROW_DEV, E, TOP, CAP, 2))(routes_keys, routes_turns).reshape((ROWS, TOP))
    placement = jax.random.permutation(key_list[6], E).astype(jnp.int32)
    router_weight = bell_draw(key_list[7], (D, E), D ** -0.5, 0.109375)
    w_up = bell_draw(key_list[8], (E, D, F), D ** -0.5, 0.109375, ((0, 4), (2, 4)))
    w_down = noise_with(key_list[9], (E, F, D), F ** -0.5, 0.109375, ((0, 4), (1, 4)), (1, 2, 4, 2.0))
    return dict(tokens=tokens, queries=queries, kv_cache=kv_cache, new_kv=new_kv, lengths=lengths, routes=routes, placement=placement, router_weight=router_weight, w_up=w_up, w_down=w_down)


EPSILON = 1e-05

def attend(tokens, queries, kv_cache, new_kv, lengths):
    per_key = QH // KVH
    score_scale = 1.0 / HD ** 0.5
    query_heads = queries.astype(jnp.float32).reshape(ROWS, KVH, per_key, HD)
    cached_keys = kv_cache[0].astype(jnp.float32)
    cached_values = kv_cache[1].astype(jnp.float32)
    scores = jnp.einsum('rgqd,rgjd->rgqj', query_heads, cached_keys) * score_scale
    fresh_key = new_kv[0].astype(jnp.float32).reshape(ROWS, KVH, HD)
    fresh_value = new_kv[1].astype(jnp.float32).reshape(ROWS, KVH, HD)
    own_score = jnp.einsum('rgqd,rgd->rgq', query_heads, fresh_key) * score_scale
    visible = jnp.arange(CTX, dtype=jnp.int32)[None, None, None, :] < lengths[:, None, None, None]
    weights = jnp.where(visible, jnp.exp(scores), 0.0)
    own_weight = jnp.exp(own_score)
    denominator = lax.optimization_barrier(jnp.sum(weights, -1)) + own_weight
    attention_probs = lax.optimization_barrier((weights / denominator[..., None]).astype(jnp.bfloat16))
    own_prob = lax.optimization_barrier((own_weight / denominator).astype(jnp.bfloat16))
    attended = jnp.einsum('rgqj,rgjd->rgqd', attention_probs.astype(jnp.float32), cached_values)
    attended = attended + own_prob.astype(jnp.float32)[..., None] * fresh_value[:, :, None, :]
    return (tokens.astype(jnp.float32) + attended.reshape(ROWS, D)).astype(jnp.bfloat16)

def reference(tokens, queries, kv_cache, new_kv, lengths, routes, placement, router_weight, w_up, w_down):
    hidden_state = attend(tokens, queries, kv_cache, new_kv, lengths)
    wide_state = hidden_state.astype(jnp.float32)
    square_sum = lax.optimization_barrier(jnp.sum(wide_state * wide_state, -1))
    raw_logits = jnp.dot(hidden_state, router_weight, preferred_element_type=jnp.float32)
    inverse = lax.rsqrt(square_sum / D + EPSILON)
    logits = raw_logits * inverse[:, None]
    normed = (wide_state * inverse[:, None]).astype(jnp.bfloat16)
    chosen = jnp.take_along_axis(logits, routes, axis=1)
    gate_exp = jnp.exp(chosen)
    gate_values = gate_exp / lax.optimization_barrier(jnp.sum(gate_exp, -1, keepdims=True))
    blocks = ROWS // ROW_DEV
    flat_routes = routes.reshape(blocks, ROW_DEV * TOP)
    onehot = (flat_routes[:, :, None] == jnp.arange(E, dtype=jnp.int32)[None, None, :]).astype(jnp.int32)
    earlier = jnp.cumsum(onehot, axis=1) - onehot
    position = lax.optimization_barrier(jnp.sum(onehot * earlier, -1)).astype(jnp.int32)
    slot_index = placement[flat_routes].astype(jnp.int32)
    block_index = jnp.broadcast_to(jnp.arange(blocks, dtype=jnp.int32)[:, None], flat_routes.shape)
    source_rows = jnp.repeat(normed.reshape(blocks, ROW_DEV, D), TOP, axis=1)
    buffer = jnp.zeros((E, blocks, CAP, D), normed.dtype).at[slot_index, block_index, position].set(source_rows)

    def expert(operands):
        expert_rows, up_part, down_part = operands
        up_sums = jnp.dot(expert_rows.reshape(blocks * CAP, D), up_part, preferred_element_type=jnp.float32)
        expert_hidden = jax.nn.silu(up_sums).astype(jnp.bfloat16)
        expert_output = jnp.dot(expert_hidden, down_part, preferred_element_type=jnp.float32).astype(jnp.bfloat16)
        return expert_output.reshape(blocks, CAP, D)
    outputs = lax.map(expert, (buffer, w_up, w_down))
    picked = outputs[slot_index, block_index, position].reshape(ROWS, TOP, D)
    expert_mix = lax.optimization_barrier(jnp.sum(gate_values[:, :, None] * picked.astype(jnp.float32), 1))
    return expert_mix.astype(jnp.bfloat16)
```

```python
import functools
import math

import jax
import jax.numpy as jnp
from jax import lax
from jax.experimental import pallas as pl
from jax.experimental.pallas import tpu as pltpu
from jax.sharding import PartitionSpec as P

EPSILON = 1e-05
LANES = 128
MIB = 2**20
NT = (((1,), (1,)), ((), ()))
TN = (((0,), (0,)), ((), ()))
VMEM = pltpu.VMEM


def in_vmem(count):
    return [pl.BlockSpec(memory_space=VMEM)] * count


def in_hbm(count):
    return [pl.BlockSpec(memory_space=pl.ANY)] * count


def column_of(row, size):
    wide = jnp.broadcast_to(row, (size, size))
    at = lax.broadcasted_iota(jnp.int32, (size, size), 0)
    own = at == lax.broadcasted_iota(jnp.int32, (size, size), 1)
    return jnp.sum(jnp.where(own, wide, 0.0), axis=1, keepdims=True)


def attention_kernel(
    ahead, tokens, queries, new_kv, lengths, routes, kv, w_up, payload, *rest
):
    if ahead:
        early, cached, sems, early_sem = rest
        fetch = pltpu.make_async_copy(w_up.at[pl.ds(0, ahead)], early, early_sem)
    else:
        cached, sems = rest
    loads = [pltpu.make_async_copy(kv.at[i], cached.at[i], sems.at[i]) for i in range(2)]
    for load in loads:
        load.start()
    if ahead:
        fetch.start()
    row_count, slice_width = tokens.shape
    local_heads, context, head_width = cached.shape[2:]
    per_key = slice_width // (local_heads * head_width)
    scale = 1.0 / math.sqrt(head_width)
    span = row_count * context

    picks = jnp.zeros((row_count, LANES), jnp.float32)
    lane = lax.broadcasted_iota(jnp.int32, (row_count, LANES), 1).astype(jnp.float32)
    for k in range(routes.shape[0]):
        chosen = column_of(routes[k : k + 1, :].astype(jnp.float32), row_count)
        picks = jnp.where(lane == chosen, 1.0, picks)
    payload[:, slice_width:] = picks.astype(jnp.bfloat16)

    limit = column_of(lengths[...].astype(jnp.float32), row_count)
    row = lax.broadcasted_iota(jnp.int32, (row_count, 1), 0).astype(jnp.float32)
    first = row * context
    last = first + limit
    first = jnp.concatenate([first] * per_key, axis=0)
    last = jnp.concatenate([last] * per_key, axis=0)
    place = lax.broadcasted_iota(jnp.int32, (per_key * row_count, span), 1).astype(jnp.float32)
    visible = (place >= first) & (place < last)

    def head_columns(ref, head):
        return ref[:, head * head_width : (head + 1) * head_width]

    loads[0].wait()
    probs, own_probs = [], []
    for g in range(local_heads):
        heads = jnp.concatenate(
            [head_columns(queries, g * per_key + i) for i in range(per_key)], axis=0
        )
        keys = cached[0, :, g].reshape(span, head_width)
        scores = lax.dot_general(heads, keys, NT, preferred_element_type=jnp.float32) * scale
        fresh = new_kv[0, :, g * head_width : (g + 1) * head_width].astype(jnp.float32)
        fresh = jnp.concatenate([fresh] * per_key, axis=0)
        own = jnp.sum(heads.astype(jnp.float32) * fresh, axis=1, keepdims=True) * scale
        weights = jnp.where(visible, jnp.exp(scores), 0.0)
        own = jnp.exp(own)
        total = jnp.sum(weights, axis=1, keepdims=True) + own
        probs.append((weights / total).astype(jnp.bfloat16))
        own_probs.append((own / total).astype(jnp.bfloat16).astype(jnp.float32))
    loads[1].wait()
    for g in range(local_heads):
        values = cached[1, :, g].reshape(span, head_width)
        mixed = jnp.dot(probs[g], values, preferred_element_type=jnp.float32)
        fresh = new_kv[1, :, g * head_width : (g + 1) * head_width].astype(jnp.float32)
        for i in range(per_key):
            part = slice(i * row_count, (i + 1) * row_count)
            head = g * per_key + i
            attended = mixed[part] + own_probs[g][part] * fresh
            state = head_columns(tokens, head).astype(jnp.float32) + attended
            payload[:, head * head_width : (head + 1) * head_width] = state.astype(jnp.bfloat16)
    if ahead:
        fetch.wait()


def attend(ahead, tokens, queries, kv, new_kv, lengths, routes, w_up):
    row_count, slice_width = tokens.shape
    payload = jax.ShapeDtypeStruct((row_count, slice_width + LANES), jnp.bfloat16)
    outs = [payload]
    scratch = [VMEM(kv.shape, kv.dtype), pltpu.SemaphoreType.DMA((2,))]
    if ahead:
        outs.append(VMEM((ahead,) + w_up.shape[1:], w_up.dtype))
        scratch.append(pltpu.SemaphoreType.DMA)
    return pl.pallas_call(
        functools.partial(attention_kernel, ahead),
        out_shape=outs,
        in_specs=in_vmem(5) + in_hbm(2),
        out_specs=in_vmem(len(outs)),
        scratch_shapes=scratch,
        compiler_params=pltpu.CompilerParams(vmem_limit_bytes=16 * MIB),
        name="attention",
    )(tokens, queries, new_kv, lengths[None, :], routes.T, kv, w_up)


def stage_kernel(start, count, w_up, payload, held, sem):
    del payload
    copy = pltpu.make_async_copy(w_up.at[pl.ds(start, count)], held, sem)
    copy.start()
    copy.wait()


def stage(start, count, w_up, payload):
    nbytes = 2 * count * w_up.shape[1] * w_up.shape[2]
    return pl.pallas_call(
        functools.partial(stage_kernel, start, count),
        out_shape=VMEM((count,) + w_up.shape[1:], w_up.dtype),
        in_specs=in_hbm(2),
        out_specs=pl.BlockSpec(memory_space=VMEM),
        scratch_shapes=[pltpu.SemaphoreType.DMA],
        compiler_params=pltpu.CompilerParams(vmem_limit_bytes=MIB),
        cost_estimate=pl.CostEstimate(flops=0, bytes_accessed=2 * nbytes, transcendentals=0),
        name="stage",
    )(w_up, payload)


def chunk_width(width):
    return next(c for c in (512, 384, 256, 128) if width % c == 0)


def expert_kernel(plan, n_early, n_out, placement, router, w_up, w_down, *refs):
    pieces, places, halves, relative, n_slots = plan
    piece_refs, refs = refs[:pieces], refs[pieces:]
    early_refs, refs = refs[:n_early], refs[n_early:]
    out_refs, refs = refs[:n_out], refs[n_out:]
    state, hidden, late, ring, late_sem, ring_sems = refs
    rows, width = state.shape
    slice_width = width // halves
    local_experts, units, _ = w_up.shape
    experts = router.shape[0]
    ae = lax.axis_index("ae")
    tp = lax.axis_index("tp") if relative else 0

    def half_start(half):
        return pl.multiple_of((tp ^ half if relative else half) * slice_width, LANES)

    n_late = late.shape[0]
    fetch = pltpu.make_async_copy(w_up.at[pl.ds(local_experts - n_late, n_late)], late, late_sem)
    fetch.start()
    step = ring.shape[2]
    per_half = slice_width // step
    chunks = halves * per_half

    def load(i):
        half = halves - 1 - i // per_half
        start = pl.multiple_of(half_start(half) + (i % per_half) * step, LANES)
        slot = i % n_slots
        return pltpu.make_async_copy(
            w_down.at[:, pl.ds(start, step)], ring.at[slot], ring_sems.at[slot]
        )

    for i in range(min(n_slots, chunks)):
        load(i).start()

    picks = [None] * (rows // 16)
    for ref, spots in zip(piece_refs, places):
        for index, block, half in spots:
            value = ref[...] if index is None else ref[index]
            state[block * 16 : (block + 1) * 16, pl.ds(half_start(half), slice_width)] = value[
                :, :slice_width
            ]
            picks[block] = value[:, slice_width:]
    picked = jnp.concatenate(picks, axis=0).astype(jnp.float32).T[:experts]
    squares = jnp.zeros((rows, LANES), jnp.float32)
    for i in range(width // LANES):
        part = state[:, i * LANES : (i + 1) * LANES].astype(jnp.float32)
        squares = squares + part * part
    square_sum = jnp.sum(squares.T, axis=0, keepdims=True)
    inverse = lax.rsqrt(square_sum / width + EPSILON)
    logits = lax.dot_general(router[...], state[...], NT, preferred_element_type=jnp.float32)
    gates = jnp.where(picked > 0.0, jnp.exp(logits * inverse), 0.0)
    gates = gates / jnp.sum(gates, axis=0, keepdims=True)

    parts = []
    for ref in early_refs:
        parts += [(ref, i) for i in range(ref.shape[0])]
    parts += [(late, i) for i in range(n_late)]
    for p, (ref, i) in enumerate(parts):
        if ref is late and i == 0:
            fetch.wait()
        gate = jnp.zeros((1, rows), jnp.float32)
        for e in range(experts):
            gate = jnp.where(placement[e] == ae * local_experts + p, gates[e : e + 1], gate)
        up = lax.dot_general(ref[i], state[...], NT, preferred_element_type=jnp.float32)
        up = up * inverse
        act = up / (1.0 + jnp.exp(-up)) * gate
        hidden[p * units : (p + 1) * units, :] = act.astype(jnp.bfloat16)

    shares = rows // n_out
    for i in range(chunks):
        load(i).wait()
        half, at = halves - 1 - i // per_half, (i % per_half) * step
        total = lax.dot_general(
            hidden[...], ring[i % n_slots], TN, preferred_element_type=jnp.float32
        )
        if i + n_slots < chunks:
            load(i + n_slots).start()
        for n, out in enumerate(out_refs):
            out[half, :, at : at + step] = total[n * shares : (n + 1) * shares].astype(out.dtype)


def run_experts(plan, out_types, placement, router, w_up, w_down, pieces, early, rows):
    halves = plan[2]
    local_experts, units, width = w_up.shape
    n_late = local_experts - sum(e.shape[0] for e in early)
    step = chunk_width(width // halves)
    n_out = len(out_types)
    scratch = [
        VMEM((rows, width), jnp.bfloat16),
        VMEM((local_experts * units, rows), jnp.bfloat16),
        VMEM((n_late, units, width), jnp.bfloat16),
        VMEM((plan[4], local_experts * units, step), jnp.bfloat16),
        pltpu.SemaphoreType.DMA,
        pltpu.SemaphoreType.DMA((plan[4],)),
    ]
    return pl.pallas_call(
        functools.partial(expert_kernel, plan, len(early), n_out),
        out_shape=[
            jax.ShapeDtypeStruct((halves, rows // n_out, width // halves), t) for t in out_types
        ],
        in_specs=[pl.BlockSpec(memory_space=pltpu.SMEM)]
        + in_vmem(1)
        + in_hbm(2)
        + in_vmem(len(pieces) + len(early)),
        out_specs=in_vmem(n_out),
        scratch_shapes=scratch,
        compiler_params=pltpu.CompilerParams(vmem_limit_bytes=37 * MIB),
        name="experts",
    )(
        placement,
        router,
        w_up,
        w_down,
        *pieces,
        *[pltpu.with_memory_space_constraint(e, VMEM) for e in early],
    )


def pair_kernel(mine, other, kept, *sent):
    halves, rows, _ = mine.shape
    for i in range(rows // 16):
        for half in range(halves):
            part = slice(i * 16, (i + 1) * 16)
            total = mine[half, part, :] + other[half, part, :].astype(jnp.float32)
            at = i * halves + half
            if at == 0:
                kept[...] = total
            else:
                sent[at - 1][...] = total.astype(jnp.bfloat16)


def pair_sum(mine, other):
    halves, rows, width = mine.shape
    blocks = halves * rows // 16
    outs = [jax.ShapeDtypeStruct((16, width), jnp.float32)]
    outs += [jax.ShapeDtypeStruct((16, width), jnp.bfloat16)] * (blocks - 1)
    return pl.pallas_call(
        pair_kernel,
        out_shape=outs,
        in_specs=in_vmem(2),
        out_specs=in_vmem(blocks),
        compiler_params=pltpu.CompilerParams(vmem_limit_bytes=8 * MIB),
        name="core_sum",
    )(mine, other)


def sum_kernel(kept, *refs):
    total = kept[...]
    for ref in refs[:-1]:
        total = total + ref[...].astype(jnp.float32)
    refs[-1][...] = total.astype(jnp.bfloat16)


def chip_sum(kept, received):
    return pl.pallas_call(
        sum_kernel,
        out_shape=jax.ShapeDtypeStruct(kept.shape, jnp.bfloat16),
        in_specs=in_vmem(1 + len(received)),
        out_specs=pl.BlockSpec(memory_space=VMEM),
        compiler_params=pltpu.CompilerParams(vmem_limit_bytes=4 * MIB),
        name="chip_sum",
    )(kept, *received)


def per_device(
    tokens, queries, kv_cache, new_kv, lengths, routes, placement, router_weight, w_up, w_down
):
    n_ae, n_tp, n_sub = lax.axis_size("ae"), lax.axis_size("tp"), lax.axis_size("sub")
    row_count, slice_width = tokens.shape
    local_experts, units, model_width = w_down.shape
    w_up = jnp.swapaxes(w_up, 1, 2)
    w_down = w_down.reshape(local_experts * units, model_width)
    router = router_weight.T
    rows = n_ae * n_sub * row_count

    ahead, behind = local_experts // 4, local_experts // 2
    payload, *early = attend(ahead, tokens, queries, kv_cache, new_kv, lengths, routes, w_up)

    direct = n_tp == 2 and n_sub == 2 and n_ae in (2, 4) and row_count == 16
    if not direct:
        pieces = [lax.all_gather(payload, ("ae", "sub", "tp"), axis=0)]
        blocks = n_ae * n_sub
        places = [[(b * n_tp + t, b, t) for b in range(blocks) for t in range(n_tp)]]
        plan = (1, places, n_tp, False, 2)
        if behind:
            early.append(stage(ahead, behind, w_up, payload))
        (total,) = run_experts(
            plan, [jnp.float32], placement, router, w_up, w_down, pieces, early, rows
        )
        total = total.reshape(n_tp, blocks, row_count, slice_width).swapaxes(0, 1)
        total = lax.psum_scatter(
            total.reshape(blocks * n_tp, row_count, slice_width),
            ("ae", "sub", "tp"),
            scatter_dimension=0,
            tiled=True,
        )
        return total.reshape(row_count, slice_width).astype(jnp.bfloat16)

    def swap(value, da, dt, ds):
        pairs = [
            (
                (a * n_tp + t) * n_sub + s,
                ((a ^ da) * n_tp + (t ^ dt)) * n_sub + (s ^ ds),
            )
            for a in range(n_ae)
            for t in range(n_tp)
            for s in range(n_sub)
        ]
        return lax.ppermute(value, ("ae", "tp", "sub"), pairs)

    partners = [(da, dt) for da in range(n_ae) for dt in range(n_tp)]
    near = [payload] + [swap(payload, da, dt, 0) for da, dt in partners[1:]]
    pieces = near + [swap(piece, 0, 0, 1) for piece in near]
    places = [[(None, ds * n_ae + da, dt)] for ds in range(n_sub) for da, dt in partners]
    if behind:
        early.append(stage(ahead, behind, w_up, payload))
    plan = (len(pieces), places, n_tp, True, 4)
    mine, other = run_experts(
        plan, [jnp.float32, jnp.bfloat16], placement, router, w_up, w_down, pieces, early, rows
    )
    kept, *sent = pair_sum(mine, swap(other, 0, 0, 1))
    received = [swap(part, da, dt, 0) for part, (da, dt) in zip(sent, partners[1:])]
    return chip_sum(kept, received)


def solution(mesh):
    placed = (
        P(("grp", "ae", "sub"), "tp"),
        P(("grp", "ae", "sub"), "tp"),
        P(None, ("grp", "ae", "sub"), "tp", None, None),
        P(None, ("grp", "ae", "sub"), "tp"),
        P(("grp", "ae", "sub")),
        P(("grp", "ae", "sub"), None),
        P(),
        P(),
        P("ae", None, ("tp", "sub")),
        P("ae", ("tp", "sub"), None),
    )
    return jax.shard_map(
        per_device,
        mesh=mesh,
        in_specs=placed,
        out_specs=P(("grp", "ae", "sub"), "tp"),
        check_vma=False,
    )
```

```python
import functools
import math

import jax
import jax.numpy as jnp
from jax import lax
from jax.experimental import pallas as pl
from jax.experimental.pallas import tpu as pltpu
from jax.sharding import PartitionSpec as P

EPSILON = 1e-05
LANES = 128
MIB = 2**20
NT = (((1,), (1,)), ((), ()))
TN = (((0,), (0,)), ((), ()))
VMEM = pltpu.VMEM


def in_vmem(count):
    return [pl.BlockSpec(memory_space=VMEM)] * count


def in_hbm(count):
    return [pl.BlockSpec(memory_space=pltpu.HBM)] * count


def column_of(row, size):
    wide = jnp.broadcast_to(row, (size, size))
    at = lax.broadcasted_iota(jnp.int32, (size, size), 0)
    own = at == lax.broadcasted_iota(jnp.int32, (size, size), 1)
    return jnp.sum(jnp.where(own, wide, 0.0), axis=1, keepdims=True)


def attention_kernel(n_early, *refs):
    sources, refs = refs[:7], refs[7:]
    outs, refs = refs[: 1 + (n_early > 0)], refs[1 + (n_early > 0) :]
    payload = outs[0]
    lengths, routes, tokens, queries, new_kv, cached, sems = refs
    moves = [
        (sources[0].at[0], cached.at[0]),
        (sources[1], queries),
        (sources[2], new_kv),
        (sources[5], routes),
        (sources[4], lengths),
        (sources[0].at[1], cached.at[1]),
        (sources[3], tokens),
    ]
    if n_early:
        moves.append((sources[6].at[pl.ds(0, n_early)], outs[1]))
    copies = [
        pltpu.make_async_copy(source, target, sems.at[i])
        for i, (source, target) in enumerate(moves)
    ]
    for copy in copies:
        copy.start()
    row_count, slice_width = tokens.shape
    local_heads, context, head_width = cached.shape[2:]
    per_key = slice_width // (local_heads * head_width)
    scale = 1.0 / math.sqrt(head_width)
    span = row_count * context

    for copy in copies[:5]:
        copy.wait()
    picks = jnp.zeros((row_count, LANES), jnp.float32)
    lane = lax.broadcasted_iota(jnp.int32, (row_count, LANES), 1).astype(jnp.float32)
    for k in range(routes.shape[0]):
        chosen = column_of(routes[k : k + 1, :].astype(jnp.float32), row_count)
        picks = jnp.where(lane == chosen, 1.0, picks)
    payload[:, slice_width:] = picks.astype(jnp.bfloat16)

    limit = column_of(lengths[...].astype(jnp.float32), row_count)
    row = lax.broadcasted_iota(jnp.int32, (row_count, 1), 0).astype(jnp.float32)
    first = row * context
    last = first + limit
    first = jnp.concatenate([first] * per_key, axis=0)
    last = jnp.concatenate([last] * per_key, axis=0)
    place = lax.broadcasted_iota(jnp.int32, (per_key * row_count, span), 1).astype(jnp.float32)
    visible = (place >= first) & (place < last)

    def head_columns(ref, head):
        return ref[:, head * head_width : (head + 1) * head_width]

    probs, own_probs = [], []
    for g in range(local_heads):
        heads = jnp.concatenate(
            [head_columns(queries, g * per_key + i) for i in range(per_key)], axis=0
        )
        keys = cached[0, :, g].reshape(span, head_width)
        scores = lax.dot_general(heads, keys, NT, preferred_element_type=jnp.float32) * scale
        fresh = new_kv[0, :, g * head_width : (g + 1) * head_width].astype(jnp.float32)
        fresh = jnp.concatenate([fresh] * per_key, axis=0)
        own = jnp.sum(heads.astype(jnp.float32) * fresh, axis=1, keepdims=True) * scale
        weights = jnp.where(visible, jnp.exp(scores), 0.0)
        own = jnp.exp(own)
        total = jnp.sum(weights, axis=1, keepdims=True) + own
        probs.append((weights / total).astype(jnp.bfloat16))
        own_probs.append((own / total).astype(jnp.bfloat16).astype(jnp.float32))
    for copy in copies[5:7]:
        copy.wait()
    for g in range(local_heads):
        values = cached[1, :, g].reshape(span, head_width)
        mixed = jnp.dot(probs[g], values, preferred_element_type=jnp.float32)
        fresh = new_kv[1, :, g * head_width : (g + 1) * head_width].astype(jnp.float32)
        for i in range(per_key):
            part = slice(i * row_count, (i + 1) * row_count)
            head = g * per_key + i
            attended = mixed[part] + own_probs[g][part] * fresh
            state = head_columns(tokens, head).astype(jnp.float32) + attended
            payload[:, head * head_width : (head + 1) * head_width] = state.astype(jnp.bfloat16)
    for copy in copies[7:]:
        copy.wait()


def attend(n_early, tokens, queries, kv, new_kv, lengths, routes, w_up):
    row_count, slice_width = tokens.shape
    lengths, routes = lengths[None, :], routes.T
    big = (kv, queries, new_kv, tokens, lengths, routes, w_up)
    held = (lengths, routes, tokens, queries, new_kv, kv)
    outs = [VMEM((row_count, slice_width + LANES), jnp.bfloat16)]
    if n_early:
        outs.append(VMEM((n_early, w_up.shape[1]), w_up.dtype))
    return pl.pallas_call(
        functools.partial(attention_kernel, n_early),
        out_shape=outs,
        in_specs=in_hbm(len(big)),
        out_specs=in_vmem(len(outs)),
        scratch_shapes=[VMEM(a.shape, a.dtype) for a in held] + [pltpu.SemaphoreType.DMA((8,))],
        compiler_params=pltpu.CompilerParams(vmem_limit_bytes=16 * MIB),
        name="attention",
    )(*[from_hbm(a) for a in big])


def from_hbm(value):
    return pltpu.with_memory_space_constraint(value, pltpu.HBM)


def chunk_width(width):
    return next(c for c in (512, 384, 256, 128) if width % c == 0)


def expert_kernel(plan, n_early, n_out, placement, router, w_up, w_down, *refs):
    pieces, places, halves, relative, n_slots = plan
    piece_refs, refs = refs[:pieces], refs[pieces:]
    early_refs, refs = refs[: n_early > 0], refs[n_early > 0 :]
    out_refs, refs = refs[:n_out], refs[n_out:]
    state, hidden, flat, late, ring, late_sems, ring_sems = refs
    rows, width = state.shape
    slice_width = width // halves
    total_units = w_up.shape[0]
    experts = router.shape[0]
    local_experts = experts // lax.axis_size("ae")
    units = total_units // local_experts
    ae = lax.axis_index("ae")
    tp = lax.axis_index("tp") if relative else 0

    def half_start(half):
        return pl.multiple_of((tp ^ half if relative else half) * slice_width, LANES)

    def fetch(i):
        return pltpu.make_async_copy(
            w_up.at[pl.ds(n_early + i * units, units)],
            late.at[pl.ds(i * units, units)],
            late_sems.at[i],
        )

    n_late = late.shape[0] // units
    for i in range(n_late):
        fetch(i).start()
    step = ring.shape[2]
    per_half = slice_width // step
    chunks = halves * per_half

    def load(i):
        half = halves - 1 - i // per_half
        start = pl.multiple_of(half_start(half) + (i % per_half) * step, LANES)
        slot = i % n_slots
        return pltpu.make_async_copy(
            w_down.at[:, pl.ds(start, step)], ring.at[slot], ring_sems.at[slot]
        )

    for i in range(min(n_slots, chunks)):
        load(i).start()

    picks = [None] * (rows // 16)
    for ref, spots in zip(piece_refs, places):
        for index, block, half in spots:
            value = ref[...] if index is None else ref[index]
            state[block * 16 : (block + 1) * 16, pl.ds(half_start(half), slice_width)] = value[
                :, :slice_width
            ]
            picks[block] = value[:, slice_width:]
    picked = jnp.concatenate(picks, axis=0).astype(jnp.float32).T[:experts]
    squares = jnp.zeros((rows, LANES), jnp.float32)
    for i in range(width // LANES):
        part = state[:, i * LANES : (i + 1) * LANES].astype(jnp.float32)
        squares = squares + part * part
    square_sum = jnp.sum(squares.T, axis=0, keepdims=True)
    inverse = lax.rsqrt(square_sum / width + EPSILON)
    logits = lax.dot_general(router[...], state[...], NT, preferred_element_type=jnp.float32)
    gates = jnp.where(picked > 0.0, jnp.exp(logits * inverse), 0.0)
    gates = gates / jnp.sum(gates, axis=0, keepdims=True)

    span = up_span(units)
    for p in range(local_experts):
        gate = jnp.zeros((1, rows), jnp.float32)
        for e in range(experts):
            gate = jnp.where(placement[e] == ae * local_experts + p, gates[e : e + 1], gate)
        if p * units < n_early:
            weights, base = early_refs[0], p * units
        else:
            weights, base = late, p * units - n_early
            fetch(base // units).wait()
        for start in range(0, units, span):
            up = lax.dot_general(
                weights[base + start : base + start + span],
                state[...],
                NT,
                preferred_element_type=jnp.float32,
            )
            up = up * inverse
            act = up / (1.0 + jnp.exp(-up)) * gate
            at = p * units + start
            hidden[at : at + span, :] = act.astype(jnp.bfloat16)
    flat[...] = hidden[...].T

    shares = rows // n_out
    for i in range(chunks):
        load(i).wait()
        half, at = halves - 1 - i // per_half, (i % per_half) * step
        total = jnp.dot(flat[...], ring[i % n_slots], preferred_element_type=jnp.float32)
        if i + n_slots < chunks:
            load(i + n_slots).start()
        for n, out in enumerate(out_refs):
            out[half, :, at : at + step] = total[n * shares : (n + 1) * shares].astype(out.dtype)


def up_span(units):
    return 336 if units % 336 == 0 else units


def run_experts(plan, n_early, out_types, placement, router, w_up, w_down, pieces, early, rows):
    halves = plan[2]
    total_units, width = w_up.shape
    local_experts = router.shape[0] // lax.axis_size("ae")
    units = total_units // local_experts
    step = chunk_width(width // halves)
    n_out = len(out_types)
    scratch = [
        VMEM((rows, width), jnp.bfloat16),
        VMEM((total_units, rows), jnp.bfloat16),
        VMEM((rows, total_units), jnp.bfloat16),
        VMEM((total_units - n_early, width), jnp.bfloat16),
        VMEM((plan[4], total_units, step), jnp.bfloat16),
        pltpu.SemaphoreType.DMA(((total_units - n_early) // units,)),
        pltpu.SemaphoreType.DMA((plan[4],)),
    ]
    return pl.pallas_call(
        functools.partial(expert_kernel, plan, n_early, n_out),
        out_shape=[VMEM((halves, rows // n_out, width // halves), t) for t in out_types],
        in_specs=[pl.BlockSpec(memory_space=pltpu.SMEM)]
        + in_vmem(1)
        + in_hbm(2)
        + in_vmem(len(pieces) + len(early)),
        out_specs=in_vmem(n_out),
        scratch_shapes=scratch,
        compiler_params=pltpu.CompilerParams(vmem_limit_bytes=50 * MIB),
        name="experts",
    )(
        placement,
        router,
        from_hbm(w_up),
        from_hbm(w_down),
        *pieces,
        *[pltpu.with_memory_space_constraint(e, VMEM) for e in early],
    )


def pair_kernel(mine, other, kept, *sent):
    halves, rows, _ = mine.shape
    for i in range(rows // 16):
        for half in range(halves):
            part = slice(i * 16, (i + 1) * 16)
            total = mine[half, part, :] + other[half, part, :].astype(jnp.float32)
            at = i * halves + half
            if at == 0:
                kept[...] = total
            else:
                sent[at - 1][...] = total.astype(jnp.bfloat16)


def pair_sum(mine, other):
    halves, rows, width = mine.shape
    blocks = halves * rows // 16
    outs = [jax.ShapeDtypeStruct((16, width), jnp.float32)]
    outs += [jax.ShapeDtypeStruct((16, width), jnp.bfloat16)] * (blocks - 1)
    return pl.pallas_call(
        pair_kernel,
        out_shape=outs,
        in_specs=in_vmem(2),
        out_specs=in_vmem(blocks),
        compiler_params=pltpu.CompilerParams(vmem_limit_bytes=8 * MIB),
        name="core_sum",
    )(mine, other)


def sum_kernel(kept, *refs):
    total = kept[...]
    for ref in refs[:-1]:
        total = total + ref[...].astype(jnp.float32)
    refs[-1][...] = total.astype(jnp.bfloat16)


def chip_sum(kept, received):
    return pl.pallas_call(
        sum_kernel,
        out_shape=jax.ShapeDtypeStruct(kept.shape, jnp.bfloat16),
        in_specs=in_vmem(1 + len(received)),
        out_specs=pl.BlockSpec(memory_space=VMEM),
        compiler_params=pltpu.CompilerParams(vmem_limit_bytes=4 * MIB),
        name="chip_sum",
    )(kept, *received)


def per_device(
    tokens, queries, kv_cache, new_kv, lengths, routes, placement, router_weight, w_up, w_down
):
    n_ae, n_tp, n_sub = lax.axis_size("ae"), lax.axis_size("tp"), lax.axis_size("sub")
    row_count, slice_width = tokens.shape
    local_experts, units, model_width = w_down.shape
    w_up = jnp.swapaxes(w_up, 1, 2).reshape(local_experts * units, model_width)
    w_down = w_down.reshape(local_experts * units, model_width)
    router = router_weight.T
    rows = n_ae * n_sub * row_count

    n_early = local_experts // 4 * units
    payload, *early = attend(
        n_early, tokens, queries, kv_cache, new_kv, lengths, routes, w_up
    )

    direct = n_tp == 2 and n_sub == 2 and n_ae in (2, 4) and row_count == 16
    if not direct:
        pieces = [lax.all_gather(payload, ("ae", "sub", "tp"), axis=0)]
        blocks = n_ae * n_sub
        places = [[(b * n_tp + t, b, t) for b in range(blocks) for t in range(n_tp)]]
        plan = (1, places, n_tp, False, 2)
        (total,) = run_experts(
            plan, n_early, [jnp.float32], placement, router, w_up, w_down, pieces, early, rows
        )
        total = total.reshape(n_tp, blocks, row_count, slice_width).swapaxes(0, 1)
        total = lax.psum_scatter(
            total.reshape(blocks * n_tp, row_count, slice_width),
            ("ae", "sub", "tp"),
            scatter_dimension=0,
            tiled=True,
        )
        return total.reshape(row_count, slice_width).astype(jnp.bfloat16)

    def swap(value, da, dt, ds):
        pairs = [
            (
                (a * n_tp + t) * n_sub + s,
                ((a ^ da) * n_tp + (t ^ dt)) * n_sub + (s ^ ds),
            )
            for a in range(n_ae)
            for t in range(n_tp)
            for s in range(n_sub)
        ]
        return lax.ppermute(value, ("ae", "tp", "sub"), pairs)

    partners = [(da, dt) for da in range(n_ae) for dt in range(n_tp)]
    near = [payload] + [swap(payload, da, dt, 0) for da, dt in partners[1:]]
    pieces = near + [swap(piece, 0, 0, 1) for piece in near]
    places = [[(None, ds * n_ae + da, dt)] for ds in range(n_sub) for da, dt in partners]
    plan = (len(pieces), places, n_tp, True, 4)
    types = [jnp.float32, jnp.bfloat16]
    mine, other = run_experts(
        plan, n_early, types, placement, router, w_up, w_down, pieces, early, rows
    )
    kept, *sent = pair_sum(mine, swap(other, 0, 0, 1))
    received = [swap(part, da, dt, 0) for part, (da, dt) in zip(sent, partners[1:])]
    return chip_sum(kept, received)


def solution(mesh):
    placed = (
        P(("grp", "ae", "sub"), "tp"),
        P(("grp", "ae", "sub"), "tp"),
        P(None, ("grp", "ae", "sub"), "tp", None, None),
        P(None, ("grp", "ae", "sub"), "tp"),
        P(("grp", "ae", "sub")),
        P(("grp", "ae", "sub"), None),
        P(),
        P(),
        P("ae", None, ("tp", "sub")),
        P("ae", ("tp", "sub"), None),
    )
    return jax.shard_map(
        per_device,
        mesh=mesh,
        in_specs=placed,
        out_specs=P(("grp", "ae", "sub"), "tp"),
        check_vma=False,
    )
```

```python
import functools
import math

import jax
import jax.numpy as jnp
from jax import lax
from jax.experimental import pallas as pl
from jax.experimental.pallas import tpu as pltpu
from jax.sharding import PartitionSpec as P

EPSILON = 1e-05
LANES = 128
MIB = 2**20
NT = (((1,), (1,)), ((), ()))
TN = (((0,), (0,)), ((), ()))
VMEM = pltpu.VMEM


def in_vmem(count):
    return [pl.BlockSpec(memory_space=VMEM)] * count


def in_hbm(count):
    return [pl.BlockSpec(memory_space=pltpu.HBM)] * count


def column_of(row, size):
    wide = jnp.broadcast_to(row, (size, size))
    at = lax.broadcasted_iota(jnp.int32, (size, size), 0)
    own = at == lax.broadcasted_iota(jnp.int32, (size, size), 1)
    return jnp.sum(jnp.where(own, wide, 0.0), axis=1, keepdims=True)


def attention_kernel(n_early, *refs):
    sources, refs = refs[:7], refs[7:]
    outs, refs = refs[: 1 + (n_early > 0)], refs[1 + (n_early > 0) :]
    payload = outs[0]
    lengths, routes, tokens, queries, new_kv, cached, sems = refs
    moves = [
        (sources[0].at[0], cached.at[0]),
        (sources[1], queries),
        (sources[2], new_kv),
        (sources[5], routes),
        (sources[4], lengths),
        (sources[0].at[1], cached.at[1]),
        (sources[3], tokens),
    ]
    if n_early:
        moves.append((sources[6].at[pl.ds(0, n_early)], outs[1]))
    copies = [
        pltpu.make_async_copy(source, target, sems.at[i])
        for i, (source, target) in enumerate(moves)
    ]
    for copy in copies:
        copy.start()
    row_count, slice_width = tokens.shape
    local_heads, context, head_width = cached.shape[2:]
    per_key = slice_width // (local_heads * head_width)
    scale = 1.0 / math.sqrt(head_width)
    span = row_count * context

    for copy in copies[:5]:
        copy.wait()
    picks = jnp.zeros((row_count, LANES), jnp.float32)
    lane = lax.broadcasted_iota(jnp.int32, (row_count, LANES), 1).astype(jnp.float32)
    for k in range(routes.shape[0]):
        chosen = column_of(routes[k : k + 1, :].astype(jnp.float32), row_count)
        picks = jnp.where(lane == chosen, 1.0, picks)
    payload[:, slice_width:] = picks.astype(jnp.bfloat16)

    limit = column_of(lengths[...].astype(jnp.float32), row_count)
    row = lax.broadcasted_iota(jnp.int32, (row_count, 1), 0).astype(jnp.float32)
    first = row * context
    last = first + limit
    first = jnp.concatenate([first] * per_key, axis=0)
    last = jnp.concatenate([last] * per_key, axis=0)
    place = lax.broadcasted_iota(jnp.int32, (per_key * row_count, span), 1).astype(jnp.float32)
    visible = (place >= first) & (place < last)

    def head_columns(ref, head):
        return ref[:, head * head_width : (head + 1) * head_width]

    probs, own_probs = [], []
    for g in range(local_heads):
        heads = jnp.concatenate(
            [head_columns(queries, g * per_key + i) for i in range(per_key)], axis=0
        )
        keys = cached[0, :, g].reshape(span, head_width)
        scores = lax.dot_general(heads, keys, NT, preferred_element_type=jnp.float32) * scale
        fresh = new_kv[0, :, g * head_width : (g + 1) * head_width].astype(jnp.float32)
        fresh = jnp.concatenate([fresh] * per_key, axis=0)
        own = jnp.sum(heads.astype(jnp.float32) * fresh, axis=1, keepdims=True) * scale
        weights = jnp.where(visible, jnp.exp(scores), 0.0)
        own = jnp.exp(own)
        total = jnp.sum(weights, axis=1, keepdims=True) + own
        probs.append((weights / total).astype(jnp.bfloat16))
        own_probs.append((own / total).astype(jnp.bfloat16).astype(jnp.float32))
    for copy in copies[5:7]:
        copy.wait()
    for g in range(local_heads):
        values = cached[1, :, g].reshape(span, head_width)
        mixed = jnp.dot(probs[g], values, preferred_element_type=jnp.float32)
        fresh = new_kv[1, :, g * head_width : (g + 1) * head_width].astype(jnp.float32)
        for i in range(per_key):
            part = slice(i * row_count, (i + 1) * row_count)
            head = g * per_key + i
            attended = mixed[part] + own_probs[g][part] * fresh
            state = head_columns(tokens, head).astype(jnp.float32) + attended
            payload[:, head * head_width : (head + 1) * head_width] = state.astype(jnp.bfloat16)
    for copy in copies[7:]:
        copy.wait()


def attend(n_early, tokens, queries, kv, new_kv, lengths, routes, w_up):
    row_count, slice_width = tokens.shape
    lengths, routes = lengths[None, :], routes.T
    big = (kv, queries, new_kv, tokens, lengths, routes, w_up)
    held = (lengths, routes, tokens, queries, new_kv, kv)
    outs = [VMEM((row_count, slice_width + LANES), jnp.bfloat16)]
    if n_early:
        outs.append(VMEM((n_early, w_up.shape[1]), w_up.dtype))
    return pl.pallas_call(
        functools.partial(attention_kernel, n_early),
        out_shape=outs,
        in_specs=in_hbm(len(big)),
        out_specs=in_vmem(len(outs)),
        scratch_shapes=[VMEM(a.shape, a.dtype) for a in held] + [pltpu.SemaphoreType.DMA((8,))],
        compiler_params=pltpu.CompilerParams(vmem_limit_bytes=16 * MIB),
        name="attention",
    )(*[from_hbm(a) for a in big])


def from_hbm(value):
    return pltpu.with_memory_space_constraint(value, pltpu.HBM)


def stage_kernel(start, w_up, payload, held, sem):
    del payload
    copy = pltpu.make_async_copy(w_up.at[pl.ds(start, held.shape[0])], held, sem)
    copy.start()
    copy.wait()


def stage(start, count, w_up, payload):
    nbytes = 2 * count * w_up.shape[1]
    return pl.pallas_call(
        functools.partial(stage_kernel, start),
        out_shape=VMEM((count, w_up.shape[1]), w_up.dtype),
        in_specs=in_hbm(1) + in_vmem(1),
        out_specs=pl.BlockSpec(memory_space=VMEM),
        scratch_shapes=[pltpu.SemaphoreType.DMA],
        compiler_params=pltpu.CompilerParams(vmem_limit_bytes=MIB),
        cost_estimate=pl.CostEstimate(flops=0, bytes_accessed=2 * nbytes, transcendentals=0),
        name="stage",
    )(from_hbm(w_up), payload)


def collect_kernel(staged, *refs):
    del staged
    for i, ref in enumerate(refs[:-1]):
        refs[-1][i] = ref[...]


def collect(staged, pieces):
    first = pieces[0]
    return pl.pallas_call(
        collect_kernel,
        out_shape=VMEM((len(pieces),) + first.shape, first.dtype),
        in_specs=in_vmem(1 + len(pieces)),
        out_specs=pl.BlockSpec(memory_space=VMEM),
        compiler_params=pltpu.CompilerParams(vmem_limit_bytes=4 * MIB),
        name="collect",
    )(*[pltpu.with_memory_space_constraint(a, VMEM) for a in (staged, *pieces)])


def chunk_width(width):
    return next(c for c in (768, 512, 384, 256, 128) if width % c == 0)


def expert_kernel(plan, n_staged, n_out, placement, router, w_up, w_down, *refs):
    pieces, places, halves, relative, n_slots = plan
    piece_refs, refs = refs[:pieces], refs[pieces:]
    early_refs, refs = refs[: n_staged], refs[n_staged:]
    out_refs, refs = refs[:n_out], refs[n_out:]
    state, hidden, sums, ring, ring_sems = refs
    rows, width = state.shape
    slice_width = width // halves
    total_units = w_up.shape[0]
    experts = router.shape[0]
    local_experts = experts // lax.axis_size("ae")
    units = total_units // local_experts
    ae = lax.axis_index("ae")
    tp = lax.axis_index("tp") if relative else 0

    def half_start(half):
        return pl.multiple_of((tp ^ half if relative else half) * slice_width, LANES)

    held = [(ref, at) for ref in early_refs for at in range(0, ref.shape[0], units)]
    n_late = local_experts - len(held)
    blocks = n_late + local_experts

    def load(i):
        source, at = (w_up, len(held) + i) if i < n_late else (w_down, i - n_late)
        return pltpu.make_async_copy(
            source.at[pl.ds(at * units, units)], ring.at[i % n_slots], ring_sems.at[i % n_slots]
        )

    def next_load(i):
        if i + n_slots < blocks:
            load(i + n_slots).start()

    for i in range(min(n_slots, blocks)):
        load(i).start()

    picks = [None] * (rows // 16)
    for ref, spots in zip(piece_refs, places):
        for index, block, half in spots:
            value = ref[...] if index is None else ref[index]
            state[block * 16 : (block + 1) * 16, pl.ds(half_start(half), slice_width)] = value[
                :, :slice_width
            ]
            picks[block] = value[:, slice_width:]
    picked = jnp.concatenate(picks, axis=0).astype(jnp.float32).T[:experts]
    squares = jnp.zeros((rows, LANES), jnp.float32)
    for i in range(width // LANES):
        part = state[:, i * LANES : (i + 1) * LANES].astype(jnp.float32)
        squares = squares + part * part
    square_sum = jnp.sum(squares.T, axis=0, keepdims=True)
    inverse = lax.rsqrt(square_sum / width + EPSILON)
    logits = lax.dot_general(router[...], state[...], NT, preferred_element_type=jnp.float32)
    gates = jnp.where(picked > 0.0, jnp.exp(logits * inverse), 0.0)
    gates = gates / jnp.sum(gates, axis=0, keepdims=True)

    span = up_span(units)
    for p in range(local_experts):
        gate = jnp.zeros((1, rows), jnp.float32)
        for e in range(experts):
            gate = jnp.where(placement[e] == ae * local_experts + p, gates[e : e + 1], gate)
        if p < len(held):
            weights, base = held[p]
        else:
            weights, base = ring.at[(p - len(held)) % n_slots], 0
            load(p - len(held)).wait()
        for start in range(0, units, span):
            up = lax.dot_general(
                weights[base + start : base + start + span],
                state[...],
                NT,
                preferred_element_type=jnp.float32,
            )
            up = up * inverse
            act = up / (1.0 + jnp.exp(-up)) * gate
            at = p * units + start
            hidden[at : at + span, :] = act.astype(jnp.bfloat16)
        if p >= len(held):
            next_load(p - len(held))

    shares = rows // n_out
    step = chunk_width(slice_width)
    for p in range(local_experts):
        i = n_late + p
        load(i).wait()
        for half in range(halves):
            for at in range(0, slice_width, step):
                start = pl.multiple_of(half_start(half) + at, LANES)
                total = lax.dot_general(
                    hidden[p * units : (p + 1) * units],
                    ring[i % n_slots, :, pl.ds(start, step)],
                    TN,
                    preferred_element_type=jnp.float32,
                )
                if p > 0:
                    total = total + sums[half, :, at : at + step]
                if p < local_experts - 1:
                    sums[half, :, at : at + step] = total
                    continue
                for n, out in enumerate(out_refs):
                    share = total[n * shares : (n + 1) * shares]
                    out[half, :, at : at + step] = share.astype(out.dtype)
        next_load(i)


def up_span(units):
    return 336 if units % 336 == 0 else units


def run_experts(plan, out_types, placement, router, w_up, w_down, pieces, early, rows):
    halves = plan[2]
    total_units, width = w_up.shape
    local_experts = router.shape[0] // lax.axis_size("ae")
    units = total_units // local_experts
    n_out = len(out_types)
    scratch = [
        VMEM((rows, width), jnp.bfloat16),
        VMEM((total_units, rows), jnp.bfloat16),
        VMEM((halves, rows, width // halves), jnp.float32),
        VMEM((plan[4], units, width), jnp.bfloat16),
        pltpu.SemaphoreType.DMA((plan[4],)),
    ]
    return pl.pallas_call(
        functools.partial(expert_kernel, plan, len(early), n_out),
        out_shape=[VMEM((halves, rows // n_out, width // halves), t) for t in out_types],
        in_specs=[pl.BlockSpec(memory_space=pltpu.SMEM)]
        + in_vmem(1)
        + in_hbm(2)
        + in_vmem(len(pieces) + len(early)),
        out_specs=in_vmem(n_out),
        scratch_shapes=scratch,
        compiler_params=pltpu.CompilerParams(vmem_limit_bytes=38 * MIB),
        name="experts",
    )(
        placement,
        router,
        from_hbm(w_up),
        from_hbm(w_down),
        *pieces,
        *[pltpu.with_memory_space_constraint(e, VMEM) for e in early],
    )


def pair_kernel(mine, other, kept, *sent):
    halves, rows, _ = mine.shape
    for i in range(rows // 16):
        for half in range(halves):
            part = slice(i * 16, (i + 1) * 16)
            total = mine[half, part, :] + other[half, part, :].astype(jnp.float32)
            at = i * halves + half
            if at == 0:
                kept[...] = total
            else:
                sent[at - 1][...] = total.astype(jnp.bfloat16)


def pair_sum(mine, other):
    halves, rows, width = mine.shape
    blocks = halves * rows // 16
    outs = [jax.ShapeDtypeStruct((16, width), jnp.float32)]
    outs += [jax.ShapeDtypeStruct((16, width), jnp.bfloat16)] * (blocks - 1)
    return pl.pallas_call(
        pair_kernel,
        out_shape=outs,
        in_specs=in_vmem(2),
        out_specs=in_vmem(blocks),
        compiler_params=pltpu.CompilerParams(vmem_limit_bytes=8 * MIB),
        name="core_sum",
    )(mine, other)


def sum_kernel(kept, *refs):
    total = kept[...]
    for ref in refs[:-1]:
        total = total + ref[...].astype(jnp.float32)
    refs[-1][...] = total.astype(jnp.bfloat16)


def chip_sum(kept, received):
    return pl.pallas_call(
        sum_kernel,
        out_shape=jax.ShapeDtypeStruct(kept.shape, jnp.bfloat16),
        in_specs=in_vmem(1 + len(received)),
        out_specs=pl.BlockSpec(memory_space=VMEM),
        compiler_params=pltpu.CompilerParams(vmem_limit_bytes=4 * MIB),
        name="chip_sum",
    )(kept, *received)


def per_device(
    tokens, queries, kv_cache, new_kv, lengths, routes, placement, router_weight, w_up, w_down
):
    n_ae, n_tp, n_sub = lax.axis_size("ae"), lax.axis_size("tp"), lax.axis_size("sub")
    row_count, slice_width = tokens.shape
    local_experts, units, model_width = w_down.shape
    w_up = jnp.swapaxes(w_up, 1, 2).reshape(local_experts * units, model_width)
    w_down = w_down.reshape(local_experts * units, model_width)
    router = router_weight.T
    rows = n_ae * n_sub * row_count

    n_early = local_experts // 4 * units
    payload, *early = attend(
        n_early, tokens, queries, kv_cache, new_kv, lengths, routes, w_up
    )

    direct = n_tp == 2 and n_sub == 2 and n_ae == 4 and row_count == 16
    if not direct:
        pieces = [lax.all_gather(payload, ("ae", "sub", "tp"), axis=0)]
        blocks = n_ae * n_sub
        places = [[(b * n_tp + t, b, t) for b in range(blocks) for t in range(n_tp)]]
        plan = (1, places, n_tp, False, 2)
        (total,) = run_experts(
            plan, [jnp.float32], placement, router, w_up, w_down, pieces, early, rows
        )
        total = total.reshape(n_tp, blocks, row_count, slice_width).swapaxes(0, 1)
        total = lax.psum_scatter(
            total.reshape(blocks * n_tp, row_count, slice_width),
            ("ae", "sub", "tp"),
            scatter_dimension=0,
            tiled=True,
        )
        return total.reshape(row_count, slice_width).astype(jnp.bfloat16)

    def swap(value, da, dt, ds):
        pairs = [
            (
                (a * n_tp + t) * n_sub + s,
                ((a ^ da) * n_tp + (t ^ dt)) * n_sub + (s ^ ds),
            )
            for a in range(n_ae)
            for t in range(n_tp)
            for s in range(n_sub)
        ]
        return lax.ppermute(value, ("ae", "tp", "sub"), pairs)

    partners = [(da, dt) for da in range(n_ae) for dt in range(n_tp)]
    near = [payload] + [swap(payload, da, dt, 0) for da, dt in partners[1:]]
    staged = stage(n_early, local_experts // 4 * units, w_up, payload)
    near = collect(staged, near)
    pieces = [near, swap(near, 0, 0, 1)]
    early.append(staged)
    places = [
        [(i, ds * n_ae + da, dt) for i, (da, dt) in enumerate(partners)] for ds in range(n_sub)
    ]
    plan = (len(pieces), places, n_tp, True, 4)
    types = [jnp.float32, jnp.bfloat16]
    mine, other = run_experts(
        plan, types, placement, router, w_up, w_down, pieces, early, rows
    )
    kept, *sent = pair_sum(mine, swap(other, 0, 0, 1))
    received = [swap(part, da, dt, 0) for part, (da, dt) in zip(sent, partners[1:])]
    return chip_sum(kept, received)


def solution(mesh):
    placed = (
        P(("grp", "ae", "sub"), "tp"),
        P(("grp", "ae", "sub"), "tp"),
        P(None, ("grp", "ae", "sub"), "tp", None, None),
        P(None, ("grp", "ae", "sub"), "tp"),
        P(("grp", "ae", "sub")),
        P(("grp", "ae", "sub"), None),
        P(),
        P(),
        P("ae", None, ("tp", "sub")),
        P("ae", ("tp", "sub"), None),
    )
    return jax.shard_map(
        per_device,
        mesh=mesh,
        in_specs=placed,
        out_specs=P(("grp", "ae", "sub"), "tp"),
        check_vma=False,
    )
```

```python
import functools
import math

import jax
import jax.numpy as jnp
from jax import lax
from jax.experimental import pallas as pl
from jax.experimental.pallas import tpu as pltpu
from jax.sharding import PartitionSpec as P

EPSILON = 1e-05
LANES = 128
MIB = 2**20
NT = (((1,), (1,)), ((), ()))
TN = (((0,), (0,)), ((), ()))
VMEM = pltpu.VMEM


def in_vmem(count):
    return [pl.BlockSpec(memory_space=VMEM)] * count


def in_hbm(count):
    return [pl.BlockSpec(memory_space=pltpu.HBM)] * count


def column_of(row, size):
    wide = jnp.broadcast_to(row, (size, size))
    at = lax.broadcasted_iota(jnp.int32, (size, size), 0)
    own = at == lax.broadcasted_iota(jnp.int32, (size, size), 1)
    return jnp.sum(jnp.where(own, wide, 0.0), axis=1, keepdims=True)


def attention_kernel(n_early, *refs):
    sources, refs = refs[:7], refs[7:]
    outs, refs = refs[: 1 + (n_early > 0)], refs[1 + (n_early > 0) :]
    payload = outs[0]
    lengths, routes, tokens, queries, new_kv, cached, sems = refs
    moves = [
        (sources[0].at[0], cached.at[0]),
        (sources[1], queries),
        (sources[2], new_kv),
        (sources[5], routes),
        (sources[4], lengths),
        (sources[0].at[1], cached.at[1]),
        (sources[3], tokens),
    ]
    if n_early:
        moves.append((sources[6].at[pl.ds(0, n_early)], outs[1]))
    copies = [
        pltpu.make_async_copy(source, target, sems.at[i])
        for i, (source, target) in enumerate(moves)
    ]
    for copy in copies:
        copy.start()
    row_count, slice_width = tokens.shape
    local_heads, context, head_width = cached.shape[2:]
    per_key = slice_width // (local_heads * head_width)
    scale = 1.0 / math.sqrt(head_width)
    span = row_count * context

    for copy in copies[:5]:
        copy.wait()
    picks = jnp.zeros((row_count, LANES), jnp.float32)
    lane = lax.broadcasted_iota(jnp.int32, (row_count, LANES), 1).astype(jnp.float32)
    for k in range(routes.shape[0]):
        chosen = column_of(routes[k : k + 1, :].astype(jnp.float32), row_count)
        picks = jnp.where(lane == chosen, 1.0, picks)
    payload[:, slice_width:] = picks.astype(jnp.bfloat16)

    limit = column_of(lengths[...].astype(jnp.float32), row_count)
    row = lax.broadcasted_iota(jnp.int32, (row_count, 1), 0).astype(jnp.float32)
    first = row * context
    last = first + limit
    first = jnp.concatenate([first] * per_key, axis=0)
    last = jnp.concatenate([last] * per_key, axis=0)
    place = lax.broadcasted_iota(jnp.int32, (per_key * row_count, span), 1).astype(jnp.float32)
    visible = (place >= first) & (place < last)

    def head_columns(ref, head):
        return ref[:, head * head_width : (head + 1) * head_width]

    probs, own_probs = [], []
    for g in range(local_heads):
        heads = jnp.concatenate(
            [head_columns(queries, g * per_key + i) for i in range(per_key)], axis=0
        )
        keys = cached[0, :, g].reshape(span, head_width)
        scores = lax.dot_general(heads, keys, NT, preferred_element_type=jnp.float32) * scale
        fresh = new_kv[0, :, g * head_width : (g + 1) * head_width].astype(jnp.float32)
        fresh = jnp.concatenate([fresh] * per_key, axis=0)
        own = jnp.sum(heads.astype(jnp.float32) * fresh, axis=1, keepdims=True) * scale
        weights = jnp.where(visible, jnp.exp(scores), 0.0)
        own = jnp.exp(own)
        total = jnp.sum(weights, axis=1, keepdims=True) + own
        probs.append((weights / total).astype(jnp.bfloat16))
        own_probs.append((own / total).astype(jnp.bfloat16).astype(jnp.float32))
    for copy in copies[5:7]:
        copy.wait()
    for g in range(local_heads):
        values = cached[1, :, g].reshape(span, head_width)
        mixed = jnp.dot(probs[g], values, preferred_element_type=jnp.float32)
        fresh = new_kv[1, :, g * head_width : (g + 1) * head_width].astype(jnp.float32)
        for i in range(per_key):
            part = slice(i * row_count, (i + 1) * row_count)
            head = g * per_key + i
            attended = mixed[part] + own_probs[g][part] * fresh
            state = head_columns(tokens, head).astype(jnp.float32) + attended
            payload[:, head * head_width : (head + 1) * head_width] = state.astype(jnp.bfloat16)
    for copy in copies[7:]:
        copy.wait()


def attend(n_early, tokens, queries, kv, new_kv, lengths, routes, w_up):
    row_count, slice_width = tokens.shape
    lengths, routes = lengths[None, :], routes.T
    big = (kv, queries, new_kv, tokens, lengths, routes, w_up)
    held = (lengths, routes, tokens, queries, new_kv, kv)
    outs = [VMEM((row_count, slice_width + LANES), jnp.bfloat16)]
    if n_early:
        outs.append(VMEM((n_early, w_up.shape[1]), w_up.dtype))
    return pl.pallas_call(
        functools.partial(attention_kernel, n_early),
        out_shape=outs,
        in_specs=in_hbm(len(big)),
        out_specs=in_vmem(len(outs)),
        scratch_shapes=[VMEM(a.shape, a.dtype) for a in held] + [pltpu.SemaphoreType.DMA((8,))],
        compiler_params=pltpu.CompilerParams(vmem_limit_bytes=16 * MIB),
        name="attention",
    )(*[from_hbm(a) for a in big])


def from_hbm(value):
    return pltpu.with_memory_space_constraint(value, pltpu.HBM)


def stage_kernel(start, w_up, payload, held, sem):
    del payload
    copy = pltpu.make_async_copy(w_up.at[pl.ds(start, held.shape[0])], held, sem)
    copy.start()
    copy.wait()


def stage(start, count, w_up, payload):
    nbytes = 2 * count * w_up.shape[1]
    return pl.pallas_call(
        functools.partial(stage_kernel, start),
        out_shape=VMEM((count, w_up.shape[1]), w_up.dtype),
        in_specs=in_hbm(1) + in_vmem(1),
        out_specs=pl.BlockSpec(memory_space=VMEM),
        scratch_shapes=[pltpu.SemaphoreType.DMA],
        compiler_params=pltpu.CompilerParams(vmem_limit_bytes=MIB),
        cost_estimate=pl.CostEstimate(flops=0, bytes_accessed=2 * nbytes, transcendentals=0),
        name="stage",
    )(from_hbm(w_up), payload)


def collect_kernel(staged, *refs):
    del staged
    for i, ref in enumerate(refs[:-1]):
        refs[-1][i] = ref[...]


def collect(staged, pieces):
    first = pieces[0]
    return pl.pallas_call(
        collect_kernel,
        out_shape=VMEM((len(pieces),) + first.shape, first.dtype),
        in_specs=in_vmem(1 + len(pieces)),
        out_specs=pl.BlockSpec(memory_space=VMEM),
        compiler_params=pltpu.CompilerParams(vmem_limit_bytes=4 * MIB),
        name="collect",
    )(*[pltpu.with_memory_space_constraint(a, VMEM) for a in (staged, *pieces)])


def chunk_width(width):
    return next(c for c in (768, 512, 384, 256, 128) if width % c == 0)


def expert_kernel(plan, n_staged, n_out, placement, router, w_up, w_down, *refs):
    pieces, places, halves, relative, n_slots = plan
    piece_refs, refs = refs[:pieces], refs[pieces:]
    early_refs, refs = refs[: n_staged], refs[n_staged:]
    out_refs, refs = refs[:n_out], refs[n_out:]
    state, hidden, sums, ring, ring_sems = refs
    rows, width = state.shape
    slice_width = width // halves
    total_units = w_up.shape[0]
    experts = router.shape[0]
    local_experts = experts // lax.axis_size("ae")
    units = total_units // local_experts
    ae = lax.axis_index("ae")
    tp = lax.axis_index("tp") if relative else 0

    def half_start(half):
        return pl.multiple_of((tp ^ half if relative else half) * slice_width, LANES)

    held = [(ref, at) for ref in early_refs for at in range(0, ref.shape[0], units)]
    n_late = local_experts - len(held)
    blocks = n_late + local_experts

    def load(i):
        source, at = (w_up, len(held) + i) if i < n_late else (w_down, i - n_late)
        return pltpu.make_async_copy(
            source.at[pl.ds(at * units, units)], ring.at[i % n_slots], ring_sems.at[i % n_slots]
        )

    def next_load(i):
        if i + n_slots < blocks:
            load(i + n_slots).start()

    for i in range(min(n_slots, blocks)):
        load(i).start()

    picks = [None] * (rows // 16)
    for ref, spots in zip(piece_refs, places):
        for index, block, half in spots:
            value = ref[...] if index is None else ref[index]
            state[block * 16 : (block + 1) * 16, pl.ds(half_start(half), slice_width)] = value[
                :, :slice_width
            ]
            picks[block] = value[:, slice_width:]
    picked = jnp.concatenate(picks, axis=0).astype(jnp.float32).T[:experts]
    squares = jnp.zeros((rows, LANES), jnp.float32)
    for i in range(width // LANES):
        part = state[:, i * LANES : (i + 1) * LANES].astype(jnp.float32)
        squares = squares + part * part
    square_sum = jnp.sum(squares.T, axis=0, keepdims=True)
    inverse = lax.rsqrt(square_sum / width + EPSILON)
    logits = lax.dot_general(router[...], state[...], NT, preferred_element_type=jnp.float32)
    gates = jnp.where(picked > 0.0, jnp.exp(logits * inverse), 0.0)
    gates = gates / jnp.sum(gates, axis=0, keepdims=True)

    span = up_span(units)
    for p in range(local_experts):
        gate = jnp.zeros((1, rows), jnp.float32)
        for e in range(experts):
            gate = jnp.where(placement[e] == ae * local_experts + p, gates[e : e + 1], gate)
        if p < len(held):
            weights, base = held[p]
        else:
            weights, base = ring.at[(p - len(held)) % n_slots], 0
            load(p - len(held)).wait()
        for start in range(0, units, span):
            up = lax.dot_general(
                weights[base + start : base + start + span],
                state[...],
                NT,
                preferred_element_type=jnp.float32,
            )
            up = up * inverse
            act = up / (1.0 + jnp.exp(-up)) * gate
            at = p * units + start
            hidden[at : at + span, :] = act.astype(jnp.bfloat16)
        if p >= len(held):
            next_load(p - len(held))

    shares = rows // n_out
    step = chunk_width(slice_width)
    for p in range(local_experts):
        i = n_late + p
        load(i).wait()
        for half in range(halves):
            for at in range(0, slice_width, step):
                start = pl.multiple_of(half_start(half) + at, LANES)
                total = lax.dot_general(
                    hidden[p * units : (p + 1) * units],
                    ring[i % n_slots, :, pl.ds(start, step)],
                    TN,
                    preferred_element_type=jnp.float32,
                )
                if p > 0:
                    total = total + sums[half, :, at : at + step]
                if p < local_experts - 1:
                    sums[half, :, at : at + step] = total
                    continue
                for n, out in enumerate(out_refs):
                    share = total[n * shares : (n + 1) * shares]
                    out[half, :, at : at + step] = share.astype(out.dtype)
        next_load(i)


def up_span(units):
    return 336 if units % 336 == 0 else units


def run_experts(plan, out_types, placement, router, w_up, w_down, pieces, early, rows):
    halves = plan[2]
    total_units, width = w_up.shape
    local_experts = router.shape[0] // lax.axis_size("ae")
    units = total_units // local_experts
    n_out = len(out_types)
    scratch = [
        VMEM((rows, width), jnp.bfloat16),
        VMEM((total_units, rows), jnp.bfloat16),
        VMEM((halves, rows, width // halves), jnp.float32),
        VMEM((plan[4], units, width), jnp.bfloat16),
        pltpu.SemaphoreType.DMA((plan[4],)),
    ]
    return pl.pallas_call(
        functools.partial(expert_kernel, plan, len(early), n_out),
        out_shape=[VMEM((halves, rows // n_out, width // halves), t) for t in out_types],
        in_specs=[pl.BlockSpec(memory_space=pltpu.SMEM)]
        + in_vmem(1)
        + in_hbm(2)
        + in_vmem(len(pieces) + len(early)),
        out_specs=in_vmem(n_out),
        scratch_shapes=scratch,
        compiler_params=pltpu.CompilerParams(vmem_limit_bytes=38 * MIB),
        name="experts",
    )(
        placement,
        router,
        from_hbm(w_up),
        from_hbm(w_down),
        *pieces,
        *[pltpu.with_memory_space_constraint(e, VMEM) for e in early],
    )


def pair_kernel(mine, other, kept, *sent):
    halves, rows, _ = mine.shape
    for i in range(rows // 16):
        for half in range(halves):
            part = slice(i * 16, (i + 1) * 16)
            total = mine[half, part, :] + other[half, part, :].astype(jnp.float32)
            at = i * halves + half
            if at == 0:
                kept[...] = total
            else:
                sent[at - 1][...] = total.astype(jnp.bfloat16)


def pair_sum(mine, other):
    halves, rows, width = mine.shape
    blocks = halves * rows // 16
    outs = [jax.ShapeDtypeStruct((16, width), jnp.float32)]
    outs += [jax.ShapeDtypeStruct((16, width), jnp.bfloat16)] * (blocks - 1)
    return pl.pallas_call(
        pair_kernel,
        out_shape=outs,
        in_specs=in_vmem(2),
        out_specs=in_vmem(blocks),
        compiler_params=pltpu.CompilerParams(vmem_limit_bytes=8 * MIB),
        name="core_sum",
    )(mine, other)


def sum_kernel(kept, *refs):
    total = kept[...]
    for ref in refs[:-1]:
        total = total + ref[...].astype(jnp.float32)
    refs[-1][...] = total.astype(jnp.bfloat16)


def chip_sum(kept, received):
    return pl.pallas_call(
        sum_kernel,
        out_shape=jax.ShapeDtypeStruct(kept.shape, jnp.bfloat16),
        in_specs=in_vmem(1 + len(received)),
        out_specs=pl.BlockSpec(memory_space=VMEM),
        compiler_params=pltpu.CompilerParams(vmem_limit_bytes=4 * MIB),
        name="chip_sum",
    )(kept, *received)


def per_device(
    tokens, queries, kv_cache, new_kv, lengths, routes, placement, router_weight, w_up, w_down
):
    n_ae, n_tp, n_sub = lax.axis_size("ae"), lax.axis_size("tp"), lax.axis_size("sub")
    row_count, slice_width = tokens.shape
    local_experts, units, model_width = w_down.shape
    w_up = jnp.swapaxes(w_up, 1, 2).reshape(local_experts * units, model_width)
    w_down = w_down.reshape(local_experts * units, model_width)
    router = router_weight.T
    rows = n_ae * n_sub * row_count

    n_early = local_experts // 4 * units
    payload, *early = attend(
        n_early, tokens, queries, kv_cache, new_kv, lengths, routes, w_up
    )

    direct = n_tp == 2 and n_sub == 2 and n_ae == 4 and row_count == 16
    if not direct:
        pieces = [lax.all_gather(payload, ("ae", "sub", "tp"), axis=0)]
        blocks = n_ae * n_sub
        places = [[(b * n_tp + t, b, t) for b in range(blocks) for t in range(n_tp)]]
        plan = (1, places, n_tp, False, 2)
        (total,) = run_experts(
            plan, [jnp.float32], placement, router, w_up, w_down, pieces, early, rows
        )
        total = total.reshape(n_tp, blocks, row_count, slice_width).swapaxes(0, 1)
        total = lax.psum_scatter(
            total.reshape(blocks * n_tp, row_count, slice_width),
            ("ae", "sub", "tp"),
            scatter_dimension=0,
            tiled=True,
        )
        return total.reshape(row_count, slice_width).astype(jnp.bfloat16)

    def swap(value, da, dt, ds):
        pairs = [
            (
                (a * n_tp + t) * n_sub + s,
                ((a ^ da) * n_tp + (t ^ dt)) * n_sub + (s ^ ds),
            )
            for a in range(n_ae)
            for t in range(n_tp)
            for s in range(n_sub)
        ]
        return lax.ppermute(value, ("ae", "tp", "sub"), pairs)

    partners = [(da, dt) for da in range(n_ae) for dt in range(n_tp)]
    near = [payload] + [swap(payload, da, dt, 0) for da, dt in partners[1:]]
    staged = stage(n_early, local_experts // 4 * units, w_up, payload)
    near = collect(staged, near)
    pieces = [near, swap(near, 0, 0, 1)]
    early.append(staged)
    places = [
        [(i, ds * n_ae + da, dt) for i, (da, dt) in enumerate(partners)] for ds in range(n_sub)
    ]
    plan = (len(pieces), places, n_tp, True, 4)
    types = [jnp.float32, jnp.bfloat16]
    mine, other = run_experts(
        plan, types, placement, router, w_up, w_down, pieces, early, rows
    )
    kept, *sent = pair_sum(mine, swap(other, 0, 0, 1))
    received = [swap(part, da, dt, 0) for part, (da, dt) in zip(sent[::-1], partners[:0:-1])]
    return chip_sum(kept, received)


def solution(mesh):
    placed = (
        P(("grp", "ae", "sub"), "tp"),
        P(("grp", "ae", "sub"), "tp"),
        P(None, ("grp", "ae", "sub"), "tp", None, None),
        P(None, ("grp", "ae", "sub"), "tp"),
        P(("grp", "ae", "sub")),
        P(("grp", "ae", "sub"), None),
        P(),
        P(),
        P("ae", None, ("tp", "sub")),
        P("ae", ("tp", "sub"), None),
    )
    return jax.shard_map(
        per_device,
        mesh=mesh,
        in_specs=placed,
        out_specs=P(("grp", "ae", "sub"), "tp"),
        check_vma=False,
    )
```

```python
import functools
import math

import jax
import jax.numpy as jnp
from jax import lax
from jax.experimental import pallas as pl
from jax.experimental.pallas import tpu as pltpu
from jax.sharding import PartitionSpec as P

EPSILON = 1e-05
LANES = 128
MIB = 2**20
NT = (((1,), (1,)), ((), ()))
TN = (((0,), (0,)), ((), ()))
VMEM = pltpu.VMEM


def in_vmem(count):
    return [pl.BlockSpec(memory_space=VMEM)] * count


def in_hbm(count):
    return [pl.BlockSpec(memory_space=pltpu.HBM)] * count


def column_of(row, size):
    wide = jnp.broadcast_to(row, (size, size))
    at = lax.broadcasted_iota(jnp.int32, (size, size), 0)
    own = at == lax.broadcasted_iota(jnp.int32, (size, size), 1)
    return jnp.sum(jnp.where(own, wide, 0.0), axis=1, keepdims=True)


def attention_kernel(n_early, *refs):
    sources, refs = refs[:7], refs[7:]
    outs, refs = refs[: 1 + (n_early > 0)], refs[1 + (n_early > 0) :]
    payload = outs[0]
    lengths, routes, tokens, queries, new_kv, cached, sems = refs
    moves = [
        (sources[0].at[0], cached.at[0]),
        (sources[1], queries),
        (sources[2], new_kv),
        (sources[5], routes),
        (sources[4], lengths),
        (sources[0].at[1], cached.at[1]),
        (sources[3], tokens),
    ]
    if n_early:
        moves.append((sources[6].at[pl.ds(0, n_early)], outs[1]))
    copies = [
        pltpu.make_async_copy(source, target, sems.at[i])
        for i, (source, target) in enumerate(moves)
    ]
    for copy in copies:
        copy.start()
    row_count, slice_width = tokens.shape
    local_heads, context, head_width = cached.shape[2:]
    per_key = slice_width // (local_heads * head_width)
    scale = 1.0 / math.sqrt(head_width)
    span = row_count * context

    for copy in copies[:5]:
        copy.wait()
    picks = jnp.zeros((row_count, LANES), jnp.float32)
    lane = lax.broadcasted_iota(jnp.int32, (row_count, LANES), 1).astype(jnp.float32)
    for k in range(routes.shape[0]):
        chosen = column_of(routes[k : k + 1, :].astype(jnp.float32), row_count)
        picks = jnp.where(lane == chosen, 1.0, picks)
    payload[:, slice_width:] = picks.astype(jnp.bfloat16)

    limit = column_of(lengths[...].astype(jnp.float32), row_count)
    row = lax.broadcasted_iota(jnp.int32, (row_count, 1), 0).astype(jnp.float32)
    first = row * context
    last = first + limit
    first = jnp.concatenate([first] * per_key, axis=0)
    last = jnp.concatenate([last] * per_key, axis=0)
    place = lax.broadcasted_iota(jnp.int32, (per_key * row_count, span), 1).astype(jnp.float32)
    visible = (place >= first) & (place < last)

    def head_columns(ref, head):
        return ref[:, head * head_width : (head + 1) * head_width]

    probs, own_probs = [], []
    for g in range(local_heads):
        heads = jnp.concatenate(
            [head_columns(queries, g * per_key + i) for i in range(per_key)], axis=0
        )
        keys = cached[0, :, g].reshape(span, head_width)
        scores = lax.dot_general(heads, keys, NT, preferred_element_type=jnp.float32) * scale
        fresh = new_kv[0, :, g * head_width : (g + 1) * head_width].astype(jnp.float32)
        fresh = jnp.concatenate([fresh] * per_key, axis=0)
        own = jnp.sum(heads.astype(jnp.float32) * fresh, axis=1, keepdims=True) * scale
        weights = jnp.where(visible, jnp.exp(scores), 0.0)
        own = jnp.exp(own)
        total = jnp.sum(weights, axis=1, keepdims=True) + own
        probs.append((weights / total).astype(jnp.bfloat16))
        own_probs.append((own / total).astype(jnp.bfloat16).astype(jnp.float32))
    for copy in copies[5:7]:
        copy.wait()
    for g in range(local_heads):
        values = cached[1, :, g].reshape(span, head_width)
        mixed = jnp.dot(probs[g], values, preferred_element_type=jnp.float32)
        fresh = new_kv[1, :, g * head_width : (g + 1) * head_width].astype(jnp.float32)
        for i in range(per_key):
            part = slice(i * row_count, (i + 1) * row_count)
            head = g * per_key + i
            attended = mixed[part] + own_probs[g][part] * fresh
            state = head_columns(tokens, head).astype(jnp.float32) + attended
            payload[:, head * head_width : (head + 1) * head_width] = state.astype(jnp.bfloat16)
    for copy in copies[7:]:
        copy.wait()


def attend(n_early, tokens, queries, kv, new_kv, lengths, routes, w_up):
    row_count, slice_width = tokens.shape
    lengths, routes = lengths[None, :], routes.T
    big = (kv, queries, new_kv, tokens, lengths, routes, w_up)
    held = (lengths, routes, tokens, queries, new_kv, kv)
    outs = [VMEM((row_count, slice_width + LANES), jnp.bfloat16)]
    if n_early:
        outs.append(VMEM((n_early, w_up.shape[1]), w_up.dtype))
    return pl.pallas_call(
        functools.partial(attention_kernel, n_early),
        out_shape=outs,
        in_specs=in_hbm(len(big)),
        out_specs=in_vmem(len(outs)),
        scratch_shapes=[VMEM(a.shape, a.dtype) for a in held] + [pltpu.SemaphoreType.DMA((8,))],
        compiler_params=pltpu.CompilerParams(vmem_limit_bytes=16 * MIB),
        name="attention",
    )(*[from_hbm(a) for a in big])


def from_hbm(value):
    return pltpu.with_memory_space_constraint(value, pltpu.HBM)


def stage_kernel(start, w_up, payload, held, sem):
    del payload
    copy = pltpu.make_async_copy(w_up.at[pl.ds(start, held.shape[0])], held, sem)
    copy.start()
    copy.wait()


def stage(start, count, w_up, payload):
    nbytes = 2 * count * w_up.shape[1]
    return pl.pallas_call(
        functools.partial(stage_kernel, start),
        out_shape=VMEM((count, w_up.shape[1]), w_up.dtype),
        in_specs=in_hbm(1) + in_vmem(1),
        out_specs=pl.BlockSpec(memory_space=VMEM),
        scratch_shapes=[pltpu.SemaphoreType.DMA],
        compiler_params=pltpu.CompilerParams(vmem_limit_bytes=MIB),
        cost_estimate=pl.CostEstimate(flops=0, bytes_accessed=2 * nbytes, transcendentals=0),
        name="stage",
    )(from_hbm(w_up), payload)


def collect_kernel(staged, *refs):
    del staged
    for i, ref in enumerate(refs[:-1]):
        refs[-1][i] = ref[...]


def collect(staged, pieces):
    first = pieces[0]
    return pl.pallas_call(
        collect_kernel,
        out_shape=VMEM((len(pieces),) + first.shape, first.dtype),
        in_specs=in_vmem(1 + len(pieces)),
        out_specs=pl.BlockSpec(memory_space=VMEM),
        compiler_params=pltpu.CompilerParams(vmem_limit_bytes=4 * MIB),
        name="collect",
    )(*[pltpu.with_memory_space_constraint(a, VMEM) for a in (staged, *pieces)])


def chunk_width(width):
    return next(c for c in (768, 512, 384, 256, 128) if width % c == 0)


def expert_kernel(plan, n_staged, n_out, placement, router, w_up, w_down, *refs):
    pieces, places, halves, relative, n_slots = plan
    piece_refs, refs = refs[:pieces], refs[pieces:]
    early_refs, refs = refs[: n_staged], refs[n_staged:]
    out_refs, refs = refs[:n_out], refs[n_out:]
    state, hidden, sums, ring, ring_sems = refs
    rows, width = state.shape
    slice_width = width // halves
    total_units = w_up.shape[0]
    experts = router.shape[0]
    local_experts = experts // lax.axis_size("ae")
    units = total_units // local_experts
    ae = lax.axis_index("ae")
    tp = lax.axis_index("tp") if relative else 0

    def half_start(half):
        return pl.multiple_of((tp ^ half if relative else half) * slice_width, LANES)

    held = [(ref, at) for ref in early_refs for at in range(0, ref.shape[0], units)]
    n_late = local_experts - len(held)
    blocks = n_late + local_experts

    def load(i):
        source, at = (w_up, len(held) + i) if i < n_late else (w_down, i - n_late)
        return pltpu.make_async_copy(
            source.at[pl.ds(at * units, units)], ring.at[i % n_slots], ring_sems.at[i % n_slots]
        )

    def next_load(i):
        if i + n_slots < blocks:
            load(i + n_slots).start()

    for i in range(min(n_slots, blocks)):
        load(i).start()

    picks = [None] * (rows // 16)
    for ref, spots in zip(piece_refs, places):
        for index, block, half in spots:
            value = ref[...] if index is None else ref[index]
            state[block * 16 : (block + 1) * 16, pl.ds(half_start(half), slice_width)] = value[
                :, :slice_width
            ]
            picks[block] = value[:, slice_width:]
    picked = jnp.concatenate(picks, axis=0).astype(jnp.float32).T[:experts]
    squares = jnp.zeros((rows, LANES), jnp.float32)
    for i in range(width // LANES):
        part = state[:, i * LANES : (i + 1) * LANES].astype(jnp.float32)
        squares = squares + part * part
    square_sum = jnp.sum(squares.T, axis=0, keepdims=True)
    inverse = lax.rsqrt(square_sum / width + EPSILON)
    logits = lax.dot_general(router[...], state[...], NT, preferred_element_type=jnp.float32)
    gates = jnp.where(picked > 0.0, jnp.exp(logits * inverse), 0.0)
    gates = gates / jnp.sum(gates, axis=0, keepdims=True)

    span = up_span(units)
    for p in range(local_experts):
        gate = jnp.zeros((1, rows), jnp.float32)
        for e in range(experts):
            gate = jnp.where(placement[e] == ae * local_experts + p, gates[e : e + 1], gate)
        if p < len(held):
            weights, base = held[p]
        else:
            weights, base = ring.at[(p - len(held)) % n_slots], 0
            load(p - len(held)).wait()
        for start in range(0, units, span):
            up = lax.dot_general(
                weights[base + start : base + start + span],
                state[...],
                NT,
                preferred_element_type=jnp.float32,
            )
            up = up * inverse
            act = up / (1.0 + jnp.exp(-up)) * gate
            at = p * units + start
            hidden[at : at + span, :] = act.astype(jnp.bfloat16)
        if p >= len(held):
            next_load(p - len(held))

    shares = rows // n_out
    step = chunk_width(slice_width)
    for p in range(local_experts):
        i = n_late + p
        load(i).wait()
        for half in range(halves):
            for at in range(0, slice_width, step):
                start = pl.multiple_of(half_start(half) + at, LANES)
                total = lax.dot_general(
                    hidden[p * units : (p + 1) * units],
                    ring[i % n_slots, :, pl.ds(start, step)],
                    TN,
                    preferred_element_type=jnp.float32,
                )
                if p > 0:
                    total = total + sums[half, :, at : at + step]
                if p < local_experts - 1:
                    sums[half, :, at : at + step] = total
                    continue
                for n, out in enumerate(out_refs):
                    share = total[n * shares : (n + 1) * shares]
                    out[half, :, at : at + step] = share.astype(out.dtype)
        next_load(i)


def up_span(units):
    return 336 if units % 336 == 0 else units


def run_experts(plan, out_types, placement, router, w_up, w_down, pieces, early, rows):
    halves = plan[2]
    total_units, width = w_up.shape
    local_experts = router.shape[0] // lax.axis_size("ae")
    units = total_units // local_experts
    n_out = len(out_types)
    scratch = [
        VMEM((rows, width), jnp.bfloat16),
        VMEM((total_units, rows), jnp.bfloat16),
        VMEM((halves, rows, width // halves), jnp.float32),
        VMEM((plan[4], units, width), jnp.bfloat16),
        pltpu.SemaphoreType.DMA((plan[4],)),
    ]
    return pl.pallas_call(
        functools.partial(expert_kernel, plan, len(early), n_out),
        out_shape=[VMEM((halves, rows // n_out, width // halves), t) for t in out_types],
        in_specs=[pl.BlockSpec(memory_space=pltpu.SMEM)]
        + in_vmem(1)
        + in_hbm(2)
        + in_vmem(len(pieces) + len(early)),
        out_specs=in_vmem(n_out),
        scratch_shapes=scratch,
        compiler_params=pltpu.CompilerParams(vmem_limit_bytes=73 * MIB // 2),
        name="experts",
    )(
        placement,
        router,
        from_hbm(w_up),
        from_hbm(w_down),
        *[pltpu.with_memory_space_constraint(a, VMEM) for a in [*pieces, *early]],
    )


def pair_kernel(mine, other, kept, *sent):
    halves, rows, _ = mine.shape
    for i in range(rows // 16):
        for half in range(halves):
            part = slice(i * 16, (i + 1) * 16)
            total = mine[half, part, :] + other[half, part, :].astype(jnp.float32)
            at = i * halves + half
            if at == 0:
                kept[...] = total
            else:
                sent[at - 1][...] = total.astype(jnp.bfloat16)


def pair_sum(mine, other):
    halves, rows, width = mine.shape
    blocks = halves * rows // 16
    outs = [jax.ShapeDtypeStruct((16, width), jnp.float32)]
    outs += [jax.ShapeDtypeStruct((16, width), jnp.bfloat16)] * (blocks - 1)
    return pl.pallas_call(
        pair_kernel,
        out_shape=outs,
        in_specs=in_vmem(2),
        out_specs=in_vmem(blocks),
        compiler_params=pltpu.CompilerParams(vmem_limit_bytes=8 * MIB),
        name="core_sum",
    )(mine, other)


def sum_kernel(kept, *refs):
    total = kept[...]
    for ref in refs[:-1]:
        total = total + ref[...].astype(jnp.float32)
    refs[-1][...] = total.astype(jnp.bfloat16)


def chip_sum(kept, received):
    return pl.pallas_call(
        sum_kernel,
        out_shape=jax.ShapeDtypeStruct(kept.shape, jnp.bfloat16),
        in_specs=in_vmem(1 + len(received)),
        out_specs=pl.BlockSpec(memory_space=VMEM),
        compiler_params=pltpu.CompilerParams(vmem_limit_bytes=4 * MIB),
        name="chip_sum",
    )(kept, *received)


def per_device(
    tokens, queries, kv_cache, new_kv, lengths, routes, placement, router_weight, w_up, w_down
):
    n_ae, n_tp, n_sub = lax.axis_size("ae"), lax.axis_size("tp"), lax.axis_size("sub")
    row_count, slice_width = tokens.shape
    local_experts, units, model_width = w_down.shape
    w_up = jnp.swapaxes(w_up, 1, 2).reshape(local_experts * units, model_width)
    w_down = w_down.reshape(local_experts * units, model_width)
    router = router_weight.T
    rows = n_ae * n_sub * row_count

    n_early = local_experts // 4 * units
    payload, *early = attend(
        n_early, tokens, queries, kv_cache, new_kv, lengths, routes, w_up
    )

    direct = n_tp == 2 and n_sub == 2 and n_ae == 4 and row_count == 16
    if not direct:
        pieces = [lax.all_gather(payload, ("ae", "sub", "tp"), axis=0)]
        blocks = n_ae * n_sub
        places = [[(b * n_tp + t, b, t) for b in range(blocks) for t in range(n_tp)]]
        plan = (1, places, n_tp, False, 2)
        (total,) = run_experts(
            plan, [jnp.float32], placement, router, w_up, w_down, pieces, early, rows
        )
        total = total.reshape(n_tp, blocks, row_count, slice_width).swapaxes(0, 1)
        total = lax.psum_scatter(
            total.reshape(blocks * n_tp, row_count, slice_width),
            ("ae", "sub", "tp"),
            scatter_dimension=0,
            tiled=True,
        )
        return total.reshape(row_count, slice_width).astype(jnp.bfloat16)

    def swap(value, da, dt, ds):
        pairs = [
            (
                (a * n_tp + t) * n_sub + s,
                ((a ^ da) * n_tp + (t ^ dt)) * n_sub + (s ^ ds),
            )
            for a in range(n_ae)
            for t in range(n_tp)
            for s in range(n_sub)
        ]
        return lax.ppermute(value, ("ae", "tp", "sub"), pairs)

    partners = [(da, dt) for da in range(n_ae) for dt in range(n_tp)]
    near = [payload] + [swap(payload, da, dt, 0) for da, dt in partners[1:]]
    staged = stage(n_early, local_experts // 4 * units, w_up, payload)
    near = collect(staged, near)
    pieces = [near, swap(near, 0, 0, 1)]
    early.append(staged)
    places = [
        [(i, ds * n_ae + da, dt) for i, (da, dt) in enumerate(partners)] for ds in range(n_sub)
    ]
    plan = (len(pieces), places, n_tp, True, 4)
    types = [jnp.float32, jnp.bfloat16]
    mine, other = run_experts(
        plan, types, placement, router, w_up, w_down, pieces, early, rows
    )
    kept, *sent = pair_sum(mine, swap(other, 0, 0, 1))
    received = [swap(part, da, dt, 0) for part, (da, dt) in zip(sent[::-1], partners[:0:-1])]
    return chip_sum(kept, received)


def solution(mesh):
    placed = (
        P(("grp", "ae", "sub"), "tp"),
        P(("grp", "ae", "sub"), "tp"),
        P(None, ("grp", "ae", "sub"), "tp", None, None),
        P(None, ("grp", "ae", "sub"), "tp"),
        P(("grp", "ae", "sub")),
        P(("grp", "ae", "sub"), None),
        P(),
        P(),
        P("ae", None, ("tp", "sub")),
        P("ae", ("tp", "sub"), None),
    )
    return jax.shard_map(
        per_device,
        mesh=mesh,
        in_specs=placed,
        out_specs=P(("grp", "ae", "sub"), "tp"),
        check_vma=False,
    )
```
